1024 devices in a mesh: dp: 128 (over y, z), tensor: 8 (over x, core).
Axes of the slice: x: 4, y: 4, z: 32, core: 2. Of those that a mesh axis runs over, the one named last changes fastest.
Arguments:
- activations: bfloat16 [32768, 4096], P('dp'), may hold values from -6 to 6
- cotangents: bfloat16 [32768, 1024], P('dp', 'tensor'), may hold values from -3 to 3
- left_stats: float32 [8, 4, 1024, 1024], P('tensor', None, 'dp'), may hold values from -6 to 6
- right_stats: float32 [8, 4, 128, 128], P('tensor', None, 'dp'), may hold values from -6 to 6
- left_roots: float32 [8, 4, 1024, 1024], P('tensor', None, 'dp'), may hold values from -1 to 4
- right_roots: float32 [8, 4, 128, 128], P('tensor'), may hold values from -1 to 4
Outputs:
- update: bfloat16 [4096, 1024], P(None, 'tensor')
- left_new: float32 [8, 4, 1024, 1024], P('tensor', None, 'dp')
- right_new: float32 [8, 4, 128, 128], P('tensor', None, 'dp')
The draws below stay inside these ranges and needn't reach their ends.
All inputs are finite; a program needn't handle non-finite values.
Results may differ from the reference program's by a relative error of at most 0.0052.
Values may be sent and summed in bfloat16 or wider, within the bound.
No kernel may reach another device: no remote copies, remote signals or barrier semaphores. Data moves between devices by JAX's collectives and lax.ppermute only.
A program may use at most 32 MiB of HBM per device.

```python
import math
import jax
import jax.numpy as jnp
from jax import lax

KV = 1024
D_WIN = 4096
BLOCK = 1024
NB = 4
KVB = 128
TOKENS = 32768
N_TENSOR = 8


def root_matrix(key, number, order, spread):
    key_diag, key_off = jax.random.split(key)
    diagonal = 10.0 ** jax.random.uniform(key_diag, (number, order), jnp.float32, -spread, spread)
    off_part = jax.random.truncated_normal(key_off, -4.0, 4.0, (number, order, order), jnp.float32) * (0.5 / math.sqrt(order))
    identity = jnp.eye(order, dtype=jnp.float32)
    return off_part * (1.0 - identity) + identity * diagonal[:, :, None]


def draw_cotangents(key, part):
    key = jax.random.fold_in(key, 11)
    key_noise, key_rows, key_cols = jax.random.split(key, 3)
    full_shape = (TOKENS, KV)
    normals = jax.random.truncated_normal(key_noise, -6.0, 6.0, full_shape, jnp.float32)
    row_scale = 10.0 ** jax.random.uniform(key_rows, (TOKENS, 1), jnp.float32)
    position = jnp.arange(KV, dtype=jnp.float32)[None, :] / KV
    col_scale = 10.0 ** (0.5 * position + 0.5 * jax.random.uniform(key_cols, (1, KV), jnp.float32))
    return (normals * row_scale * col_scale / (10.0 * math.sqrt(TOKENS))).astype(jnp.bfloat16)


def draw_left_roots(key, part):
    key = jax.random.fold_in(key, 23)
    spread = 0.3
    return root_matrix(key, N_TENSOR * NB, BLOCK, spread).reshape(N_TENSOR, NB, BLOCK, BLOCK)


def draw_right_roots(key, part):
    key = jax.random.fold_in(key, 37)
    spread = 0.3
    return root_matrix(key, N_TENSOR * NB, KVB, spread).reshape(N_TENSOR, NB, KVB, KVB)


def level_of(own_key, dims, cuts, least, top_value):
    level, own = 1.0, jax.random.fold_in(own_key, 6)
    for dim, shards_of in cuts:
        steps = jnp.exp(jax.random.uniform(jax.random.fold_in(own, dim), (shards_of,), jnp.float32, least / len(cuts), top_value / len(cuts)))
        level = level * jnp.repeat(steps, dims[dim] // shards_of).reshape([-1 if axis == dim else 1 for axis in range(len(dims))])
    return level


def bell_draw(stream_key, dims, width, bound, cuts=(), held_as=jnp.bfloat16):
    entries = width * jax.random.normal(stream_key, dims, jnp.float32)
    if cuts:
        entries = entries * level_of(stream_key, dims, cuts, -0.22, 0.18)
    return jnp.clip(entries, -bound, bound).astype(held_as)


def setup_inputs(seed: int = 0) -> dict:
    keys = jax.random.split(jax.random.key(seed), 7)
    return {
        "activations": bell_draw(keys[0], (TOKENS, D_WIN), 1.0, 6.0, ((0, 128),)),
        "cotangents": draw_cotangents(jax.random.fold_in(keys[6], 71), 0),
        "left_stats": bell_draw(keys[2], (N_TENSOR, NB, BLOCK, BLOCK), 1.0, 6.0, ((0, 8), (2, 128)), jnp.float32),
        "right_stats": bell_draw(keys[3], (N_TENSOR, NB, KVB, KVB), 1.0, 6.0, ((0, 8), (2, 128)), jnp.float32),
        "left_roots": draw_left_roots(jax.random.fold_in(keys[6], 71), 0),
        "right_roots": draw_right_roots(jax.random.fold_in(keys[6], 71), 0),
    }


stat_decay = 0.95
highest = lax.Precision.HIGHEST

def reference(activations, cotangents, left_stats, right_stats, left_roots, right_roots):
    tensor_count = left_stats.shape[0]
    block_count = left_stats.shape[1]
    col_width = cotangents.shape[1] // tensor_count
    gradient = jnp.dot(activations.T, cotangents, preferred_element_type=jnp.float32)
    left_list = []
    right_list = []
    dir_list = []
    grad_sq = []
    dir_sq = []
    for tensor_pos in range(tensor_count):
        for block_pos in range(block_count):
            grad_block = gradient[block_pos * BLOCK:(block_pos + 1) * BLOCK, tensor_pos * col_width:(tensor_pos + 1) * col_width]
            left_list.append(stat_decay * left_stats[tensor_pos, block_pos] + (1.0 - stat_decay) * jnp.dot(grad_block, grad_block.T, precision=highest) / col_width)
            right_list.append(stat_decay * right_stats[tensor_pos, block_pos] + (1.0 - stat_decay) * jnp.dot(grad_block.T, grad_block, precision=highest) / BLOCK)
            mixed_rows = jnp.dot(grad_block, right_roots[tensor_pos, block_pos], precision=highest)
            direction = jnp.dot(left_roots[tensor_pos, block_pos], mixed_rows, precision=highest).astype(jnp.bfloat16)
            dir_list.append(direction)
            grad_sq.append(jnp.sum(grad_block * grad_block))
            wide_dir = direction.astype(jnp.float32)
            dir_sq.append(jnp.sum(wide_dir * wide_dir))
    layer_sq = sum_list(grad_sq)
    layer_rms = jnp.sqrt(layer_sq / (D_WIN * KV))
    columns = []
    for tensor_pos in range(tensor_count):
        stacked = []
        for block_pos in range(block_count):
            where = tensor_pos * block_count + block_pos
            factor = jnp.sqrt(grad_sq[where] / dir_sq[where]) / layer_rms
            stacked.append((dir_list[where].astype(jnp.float32) * factor).astype(jnp.bfloat16))
        columns.append(jnp.concatenate(stacked, axis=0))
    update = jnp.concatenate(columns, axis=1)
    left_new = jnp.stack(left_list).reshape(left_stats.shape)
    right_new = jnp.stack(right_list).reshape(right_stats.shape)
    return (update, left_new, right_new)

def sum_list(values):
    result = values[0]
    for other in values[1:]:
        result = result + other
    return result
```

```python
import jax
import jax.numpy as jnp
from jax import lax
from jax.sharding import Mesh, PartitionSpec as P

BLOCK = 1024
stat_decay = 0.95
highest = lax.Precision.HIGHEST
f32 = jnp.float32
bf16 = jnp.bfloat16


def everyone(piece, axis, count):
    return lax.all_to_all(
        jnp.broadcast_to(piece[None], (count, *piece.shape)), axis, 0, 0, tiled=True
    )


def shards(activations, cotangents, left_stats, right_stats, left_roots, right_roots):
    ny = lax.axis_size("y")
    nz = lax.axis_size("z")
    y = lax.axis_index("y")
    z = lax.axis_index("z")
    features = activations.shape[1]
    width = cotangents.shape[1]
    blocks = features // BLOCK
    mine = left_roots.shape[2]
    per_row = BLOCK // width

    partial = lax.dot_general(
        activations, cotangents, (((0,), (0,)), ((), ())), preferred_element_type=f32
    ).reshape(blocks, BLOCK, width)
    roots = left_roots[0]
    roots_high = roots.astype(bf16)
    roots_low = (roots - roots_high.astype(f32)).astype(bf16)
    root_rows = mine * per_row
    sent = jnp.concatenate(
        [
            partial.astype(bf16),
            roots_high.reshape(blocks, root_rows, width),
            roots_low.reshape(blocks, root_rows, width),
        ],
        axis=1,
    )
    got = lax.all_to_all(sent, "y", 0, 0, tiled=True)
    kept = lax.dynamic_index_in_dim(partial, y, 0, keepdims=False)
    others = jnp.where((jnp.arange(ny) == y)[:, None, None], 0.0, got[:, :BLOCK].astype(f32))
    column_part = kept + jnp.sum(others, axis=0)
    roots_high = got[:, BLOCK : BLOCK + root_rows].reshape(ny * mine, BLOCK)
    roots_low = got[:, BLOCK + root_rows :].reshape(ny * mine, BLOCK)

    got = lax.all_to_all(
        column_part.astype(bf16).reshape(nz, BLOCK // nz, width), "z", 0, 0, tiled=True
    )
    own = jnp.sum(got.astype(f32), axis=0).astype(bf16)
    gradient = everyone(own, "z", nz).reshape(BLOCK, width)

    inner = lax.dot_general(
        gradient, gradient, (((0,), (0,)), ((), ())), preferred_element_type=f32
    )
    wide = gradient.astype(f32)
    grad_sq = jnp.sum(wide * wide)
    layer_sq = lax.psum(grad_sq, ("y", "tensor"))
    layer_rms = jnp.sqrt(layer_sq / (features * width * lax.axis_size("tensor")))

    right = lax.dynamic_index_in_dim(right_roots[0], y, 0, keepdims=False)
    mixed = jnp.dot(roots_high, gradient, preferred_element_type=f32) + jnp.dot(
        roots_low, gradient, preferred_element_type=f32
    )
    direction = jnp.dot(mixed, right, precision=highest).astype(bf16)
    direction = everyone(direction, "z", nz).reshape(nz, ny, mine, width)
    wide = direction.astype(f32)
    dir_sq = jnp.sum(wide * wide)
    factor = jnp.sqrt(grad_sq / dir_sq) / layer_rms
    update = (wide * factor).transpose(1, 0, 2, 3).reshape(BLOCK, width).astype(bf16)

    rows = lax.dynamic_index_in_dim(gradient.reshape(ny, nz, mine, width), z, 1, keepdims=False)
    outer = lax.dot_general(
        rows.reshape(ny * mine, width), gradient, (((1,), (1,)), ((), ())), preferred_element_type=f32
    )
    outer = outer.astype(bf16).reshape(ny, root_rows, width)
    inner = lax.dynamic_index_in_dim(inner.reshape(ny, nz, width), z, 1, keepdims=True).astype(bf16)
    inner = jnp.broadcast_to(inner, (ny, 16, width))
    sent = jnp.concatenate(
        [jnp.broadcast_to(update[None], (ny, BLOCK, width)), outer, inner], axis=1
    )
    got = lax.all_to_all(sent, "y", 0, 0, tiled=True)
    update = got[:, :BLOCK].reshape(blocks * BLOCK, width)
    outer = got[:, BLOCK : BLOCK + root_rows].astype(f32).reshape(blocks, mine, BLOCK)
    inner = got[:, BLOCK + root_rows : BLOCK + root_rows + 1].astype(f32)
    left_new = stat_decay * left_stats + ((1.0 - stat_decay) / width) * outer[None]
    right_new = stat_decay * right_stats + ((1.0 - stat_decay) / BLOCK) * inner[None]
    return (update, left_new, right_new)


def solution(mesh):
    dp, tensor = mesh.devices.shape
    blocks = 4
    fine = Mesh(mesh.devices.reshape(blocks, dp // blocks, tensor), ("y", "z", "tensor"))
    dp = ("y", "z")
    in_specs = (
        P(dp, None),
        P(dp, "tensor"),
        P("tensor", None, dp, None),
        P("tensor", None, dp, None),
        P("tensor", None, dp, None),
        P("tensor", None, None, None),
    )
    out_specs = (P(None, "tensor"), P("tensor", None, dp, None), P("tensor", None, dp, None))
    return jax.shard_map(shards, mesh=fine, in_specs=in_specs, out_specs=out_specs, check_vma=False)
```

```python
import jax
import jax.numpy as jnp
from jax import lax
from jax.sharding import Mesh, PartitionSpec as P

BLOCK = 1024
stat_decay = 0.95
highest = lax.Precision.HIGHEST
f32 = jnp.float32
bf16 = jnp.bfloat16


def everyone(piece, axis, count):
    return lax.all_to_all(
        jnp.broadcast_to(piece[None], (count, *piece.shape)), axis, 0, 0, tiled=True
    )


def shards(activations, cotangents, left_stats, right_stats, left_roots, right_roots):
    ny = lax.axis_size("y")
    nz = lax.axis_size("z")
    tensors = lax.axis_size("tensor")
    y = lax.axis_index("y")
    z = lax.axis_index("z")
    features = activations.shape[1]
    width = cotangents.shape[1]
    blocks = features // BLOCK
    mine = left_roots.shape[2]
    per_row = BLOCK // width

    partial = lax.dot_general(
        activations, cotangents, (((0,), (0,)), ((), ())), preferred_element_type=f32
    ).reshape(blocks, BLOCK, width)
    root_rows = mine * per_row
    roots = left_roots[0].astype(bf16).reshape(blocks, root_rows, width)
    sent = jnp.concatenate([partial.astype(bf16), roots], axis=1)
    got = lax.all_to_all(sent, "y", 0, 0, tiled=True)
    roots = lax.all_gather(got[:, BLOCK:].reshape(ny * mine, BLOCK), "z", axis=0, tiled=True)
    kept = lax.dynamic_index_in_dim(partial, y, 0, keepdims=False)
    others = jnp.where((jnp.arange(ny) == y)[:, None, None], 0.0, got[:, :BLOCK].astype(f32))
    column_part = kept + jnp.sum(others, axis=0)

    got = lax.all_to_all(
        column_part.astype(bf16).reshape(nz, BLOCK // nz, width), "z", 0, 0, tiled=True
    )
    own = jnp.sum(got.astype(f32), axis=0).astype(bf16)
    gradient = everyone(own, "z", nz).reshape(BLOCK, width)

    inner = lax.dot_general(
        gradient, gradient, (((0,), (0,)), ((), ())), preferred_element_type=f32
    )
    wide = gradient.astype(f32)
    grad_sq = jnp.sum(wide * wide)

    right = lax.dynamic_index_in_dim(right_roots[0], y, 0, keepdims=False)
    mixed = jnp.dot(roots, gradient, preferred_element_type=f32)
    direction = jnp.dot(mixed, right, precision=highest).astype(bf16)
    wide = direction.astype(f32)
    dir_sq = jnp.sum(wide * wide)
    direction = direction.reshape(nz, ny, mine, width).transpose(1, 0, 2, 3).reshape(BLOCK, width)

    rows = lax.dynamic_index_in_dim(gradient.reshape(ny, nz, mine, width), z, 1, keepdims=False)
    outer = lax.dot_general(
        rows.reshape(ny * mine, width), gradient, (((1,), (1,)), ((), ())), preferred_element_type=f32
    )
    outer = outer.astype(bf16).reshape(ny, root_rows, width)
    inner = lax.dynamic_index_in_dim(inner.reshape(ny, nz, width), z, 1, keepdims=True).astype(bf16)
    inner = jnp.broadcast_to(inner, (ny, 16, width))
    sent = jnp.concatenate(
        [jnp.broadcast_to(direction[None], (ny, BLOCK, width)), outer, inner], axis=1
    )
    got = lax.all_to_all(sent, "y", 0, 0, tiled=True)
    norms = jnp.where((jnp.arange(8) == 0)[:, None], grad_sq, dir_sq)
    norms = everyone(jnp.broadcast_to(norms, (8, width)), ("y", "tensor"), ny * tensors)
    norms = norms[:, :2, 0].reshape(ny, tensors, 2)
    layer_rms = jnp.sqrt(jnp.sum(norms[:, :, 0]) / (features * width * tensors))
    norms = lax.dynamic_index_in_dim(norms, lax.axis_index("tensor"), 1, keepdims=False)
    factor = jnp.sqrt(norms[:, 0] / norms[:, 1]) / layer_rms
    update = (got[:, :BLOCK].astype(f32) * factor[:, None, None]).astype(bf16)
    update = update.reshape(blocks * BLOCK, width)
    outer = got[:, BLOCK : BLOCK + root_rows].astype(f32).reshape(blocks, mine, BLOCK)
    inner = got[:, BLOCK + root_rows : BLOCK + root_rows + 1].astype(f32)
    left_new = stat_decay * left_stats + ((1.0 - stat_decay) / width) * outer[None]
    right_new = stat_decay * right_stats + ((1.0 - stat_decay) / BLOCK) * inner[None]
    return (update, left_new, right_new)


def solution(mesh):
    dp, tensor = mesh.devices.shape
    blocks = 4
    fine = Mesh(mesh.devices.reshape(blocks, dp // blocks, tensor), ("y", "z", "tensor"))
    dp = ("y", "z")
    in_specs = (
        P(dp, None),
        P(dp, "tensor"),
        P("tensor", None, dp, None),
        P("tensor", None, dp, None),
        P("tensor", None, dp, None),
        P("tensor", None, None, None),
    )
    out_specs = (P(None, "tensor"), P("tensor", None, dp, None), P("tensor", None, dp, None))
    return jax.shard_map(shards, mesh=fine, in_specs=in_specs, out_specs=out_specs, check_vma=False)
```

```python
import jax
import jax.numpy as jnp
from jax import lax
from jax.sharding import Mesh, PartitionSpec as P

BLOCK = 1024
stat_decay = 0.95
highest = lax.Precision.HIGHEST
f32 = jnp.float32
bf16 = jnp.bfloat16
Z = ("far", "near")


def swap(pieces, axis):
    return lax.all_to_all(pieces, axis, 0, 0, tiled=True)


def everyone(piece, axis):
    return swap(jnp.broadcast_to(piece[None], (lax.axis_size(axis), *piece.shape)), axis)


def thirds(value):
    parts = []
    for _ in range(3):
        part = lax.reduce_precision(value, 8, 7)
        parts.append(part.astype(bf16))
        value = value - part
    return parts


def shards(activations, cotangents, left_stats, right_stats, left_roots, right_roots):
    ny = lax.axis_size("y")
    nfar = lax.axis_size("far")
    nnear = lax.axis_size("near")
    nz = nfar * nnear
    tensors = lax.axis_size("tensor")
    y = lax.axis_index("y")
    z = lax.axis_index(Z)
    features = activations.shape[1]
    width = cotangents.shape[1]
    blocks = features // BLOCK
    mine = left_roots.shape[2]
    root_rows = mine * (BLOCK // width)

    partial = lax.dot_general(
        activations, cotangents, (((0,), (0,)), ((), ())), preferred_element_type=f32
    ).reshape(blocks, BLOCK, width)
    roots = left_roots[0].astype(bf16).reshape(blocks, root_rows, width)
    got = swap(jnp.concatenate([partial.astype(bf16), roots], axis=1), "y")
    roots = got[:, BLOCK:].reshape(ny * mine, BLOCK)
    kept = lax.dynamic_index_in_dim(partial, y, 0, keepdims=False)
    others = jnp.where((jnp.arange(ny) == y)[:, None, None], 0.0, got[:, :BLOCK].astype(f32))
    column_part = kept + jnp.sum(others, axis=0)

    got = swap(column_part.astype(bf16).reshape(nnear, BLOCK // nnear, width), "near")
    got = everyone(jnp.sum(got.astype(f32), axis=0).astype(bf16), "far")
    own = jnp.sum(got.astype(f32), axis=0).astype(bf16)
    gradient = everyone(own, "near").reshape(BLOCK, width)

    inner = lax.dot_general(
        gradient, gradient, (((0,), (0,)), ((), ())), preferred_element_type=f32
    )
    wide = gradient.astype(f32)
    grad_sq = jnp.sum(wide * wide)
    block_sq = lax.psum(grad_sq, "tensor")

    right = lax.dynamic_index_in_dim(right_roots[0], y, 0, keepdims=False)
    mixed = jnp.dot(roots, gradient, preferred_element_type=f32)
    direction = jnp.dot(mixed, right, precision=highest).astype(bf16)
    direction = everyone(direction, Z).reshape(nz, ny, mine, width)
    direction = direction.transpose(1, 0, 2, 3).reshape(BLOCK, width)
    wide = direction.astype(f32)
    dir_sq = jnp.sum(wide * wide)

    rows = lax.dynamic_index_in_dim(gradient.reshape(ny, nz, mine, width), z, 1, keepdims=False)
    outer = lax.dot_general(
        rows.reshape(ny * mine, width), gradient, (((1,), (1,)), ((), ())), preferred_element_type=f32
    )
    outer = outer.astype(bf16).reshape(ny, root_rows, width)
    inner = lax.dynamic_index_in_dim(inner.reshape(ny, nz, width), z, 1, keepdims=True).astype(bf16)
    line = jnp.arange(16)[:, None]
    scalars = thirds(jnp.sqrt(grad_sq / dir_sq)) + thirds(block_sq)
    extra = jnp.broadcast_to(inner, (ny, 16, width))
    for place, scalar in enumerate(scalars, 1):
        extra = jnp.where(line == place, scalar, extra)
    got = swap(
        jnp.concatenate(
            [jnp.broadcast_to(direction[None], (ny, BLOCK, width)), outer, extra], axis=1
        ),
        "y",
    )
    extra = got[:, BLOCK + root_rows :].astype(f32)
    ratio = jnp.sum(extra[:, 1:4, 0], axis=1)
    layer_sq = jnp.sum(extra[:, 4:7, 0])
    factor = ratio / jnp.sqrt(layer_sq / (features * width * tensors))
    update = (got[:, :BLOCK].astype(f32) * factor[:, None, None]).astype(bf16)
    update = update.reshape(blocks * BLOCK, width)
    outer = got[:, BLOCK : BLOCK + root_rows].astype(f32).reshape(blocks, mine, BLOCK)
    left_new = stat_decay * left_stats + ((1.0 - stat_decay) / width) * outer[None]
    right_new = stat_decay * right_stats + ((1.0 - stat_decay) / BLOCK) * extra[None, :, :1]
    return (update, left_new, right_new)


def solution(mesh):
    dp, tensor = mesh.devices.shape
    blocks, near = 4, 8
    fine = Mesh(
        mesh.devices.reshape(blocks, dp // (blocks * near), near, tensor),
        ("y", "far", "near", "tensor"),
    )
    dp = ("y", *Z)
    in_specs = (
        P(dp, None),
        P(dp, "tensor"),
        P("tensor", None, dp, None),
        P("tensor", None, dp, None),
        P("tensor", None, dp, None),
        P("tensor", None, None, None),
    )
    out_specs = (P(None, "tensor"), P("tensor", None, dp, None), P("tensor", None, dp, None))
    return jax.shard_map(shards, mesh=fine, in_specs=in_specs, out_specs=out_specs, check_vma=False)
```

```python
import jax
import jax.numpy as jnp
from jax import lax
from jax.sharding import Mesh, PartitionSpec as P

BLOCK = 1024
stat_decay = 0.95
highest = lax.Precision.HIGHEST
f32 = jnp.float32
bf16 = jnp.bfloat16
Z = ("far", "near")


def swap(pieces, axis):
    return lax.all_to_all(pieces, axis, 0, 0, tiled=True)


def everyone(piece, axis):
    return swap(jnp.broadcast_to(piece[None], (lax.axis_size(axis), *piece.shape)), axis)


def thirds(value):
    parts = []
    for _ in range(3):
        part = lax.reduce_precision(value, 8, 7)
        parts.append(part.astype(bf16))
        value = value - part
    return parts


def shards(activations, cotangents, left_stats, right_stats, left_roots, right_roots):
    ny = lax.axis_size("y")
    nfar = lax.axis_size("far")
    nnear = lax.axis_size("near")
    nz = nfar * nnear
    tensors = lax.axis_size("tensor")
    y = lax.axis_index("y")
    z = lax.axis_index(Z)
    features = activations.shape[1]
    width = cotangents.shape[1]
    blocks = features // BLOCK
    mine = left_roots.shape[2]
    root_rows = mine * (BLOCK // width)

    partial = lax.dot_general(
        activations, cotangents, (((0,), (0,)), ((), ())), preferred_element_type=f32
    ).reshape(blocks, BLOCK, width)
    roots = left_roots[0].astype(bf16).reshape(blocks, root_rows, width)
    got = swap(jnp.concatenate([partial.astype(bf16), roots], axis=1), "y")
    roots = got[:, BLOCK:].reshape(ny * mine, BLOCK)
    kept = lax.dynamic_index_in_dim(partial, y, 0, keepdims=False)
    others = jnp.where((jnp.arange(ny) == y)[:, None, None], 0.0, got[:, :BLOCK].astype(f32))
    column_part = kept + jnp.sum(others, axis=0)

    far = lax.axis_index("far")
    held = [roots]

    def step(operand, transfer):
        operand, block = lax.optimization_barrier((operand, roots))
        turn = [(i, (i + len(held)) % nfar) for i in range(nfar)]
        held.append(lax.ppermute(block, "far", turn))
        got = transfer(operand)
        if len(held) > 2:
            got, held[-2] = lax.optimization_barrier((got, held[-2]))
        return got

    pieces = column_part.astype(bf16).reshape(nnear, BLOCK // nnear, width)
    got = step(pieces, lambda pieces: swap(pieces, "near"))
    part = jnp.sum(got.astype(f32), axis=0).astype(bf16)
    got = step(part, lambda part: everyone(part, "far"))
    own = jnp.sum(got.astype(f32), axis=0).astype(bf16)
    gradient = step(own, lambda own: everyone(own, "near")).reshape(BLOCK, width)
    roots = jnp.concatenate(held, axis=0)

    inner = lax.dot_general(
        gradient, gradient, (((0,), (0,)), ((), ())), preferred_element_type=f32
    )
    wide = gradient.astype(f32)
    grad_sq = jnp.sum(wide * wide, axis=0)
    block_sq = lax.psum(grad_sq, "tensor")

    right = lax.dynamic_index_in_dim(right_roots[0], y, 0, keepdims=False)
    mixed = jnp.dot(roots, gradient, preferred_element_type=f32)
    direction = jnp.dot(mixed, right, precision=highest).reshape(1, nfar, ny * mine, width)
    steps = jnp.arange(nfar)
    turned = (far - steps[:, None]) % nfar == steps[None, :]
    direction = jnp.sum(jnp.where(turned[:, :, None, None], direction, 0.0), axis=1).astype(bf16)
    direction = everyone(direction, "near").reshape(nnear, nfar, ny, mine, width)
    direction = direction.transpose(2, 1, 0, 3, 4).reshape(BLOCK, width)
    wide = direction.astype(f32)
    dir_sq = jnp.sum(wide * wide, axis=0)

    rows = lax.dynamic_index_in_dim(gradient.reshape(ny, nz, mine, width), z, 1, keepdims=False)
    outer = lax.dot_general(
        rows.reshape(ny * mine, width), gradient, (((1,), (1,)), ((), ())), preferred_element_type=f32
    )
    outer = outer.astype(bf16).reshape(ny, root_rows, width)
    inner = lax.dynamic_index_in_dim(inner.reshape(ny, nz, width), z, 1, keepdims=True).astype(bf16)
    line = jnp.arange(16)[:, None]
    extra = jnp.broadcast_to(inner, (ny, 16, width))
    for place, values in enumerate(thirds(grad_sq) + thirds(dir_sq) + thirds(block_sq), 1):
        extra = jnp.where(line == place, values, extra)
    got = swap(
        jnp.concatenate(
            [jnp.broadcast_to(direction[None], (ny, BLOCK, width)), outer, extra], axis=1
        ),
        "y",
    )
    extra = got[:, BLOCK + root_rows :].astype(f32)
    grad_sq, dir_sq, block_sq = (
        jnp.sum(extra[:, 1 + 3 * n : 4 + 3 * n], axis=(1, 2), keepdims=True) for n in range(3)
    )
    layer_sq = jnp.sum(block_sq, axis=0, keepdims=True)
    factor = jnp.sqrt(grad_sq / dir_sq) / jnp.sqrt(layer_sq / (features * width * tensors))
    update = (got[:, :BLOCK].astype(f32) * factor).astype(bf16)
    update = update.reshape(blocks * BLOCK, width)
    outer = got[:, BLOCK : BLOCK + root_rows].astype(f32).reshape(blocks, mine, BLOCK)
    left_new = stat_decay * left_stats + ((1.0 - stat_decay) / width) * outer[None]
    right_new = stat_decay * right_stats + ((1.0 - stat_decay) / BLOCK) * extra[None, :, :1]
    return (update, left_new, right_new)


def solution(mesh):
    dp, tensor = mesh.devices.shape
    blocks, near = 4, 8
    fine = Mesh(
        mesh.devices.reshape(blocks, dp // (blocks * near), near, tensor),
        ("y", "far", "near", "tensor"),
    )
    dp = ("y", *Z)
    in_specs = (
        P(dp, None),
        P(dp, "tensor"),
        P("tensor", None, dp, None),
        P("tensor", None, dp, None),
        P("tensor", None, dp, None),
        P("tensor", None, None, None),
    )
    out_specs = (P(None, "tensor"), P("tensor", None, dp, None), P("tensor", None, dp, None))
    return jax.shard_map(shards, mesh=fine, in_specs=in_specs, out_specs=out_specs, check_vma=False)
```

```python
import jax
import jax.numpy as jnp
from jax import lax
from jax.sharding import Mesh, PartitionSpec as P

BLOCK = 1024
stat_decay = 0.95
highest = lax.Precision.HIGHEST
f32 = jnp.float32
bf16 = jnp.bfloat16
Z = ("far", "near")


def swap(pieces, axis):
    return lax.all_to_all(pieces, axis, 0, 0, tiled=True)


def everyone(piece, axis):
    return swap(jnp.broadcast_to(piece[None], (lax.axis_size(axis), *piece.shape)), axis)


def thirds(value):
    parts = []
    for _ in range(3):
        part = lax.reduce_precision(value, 8, 7)
        parts.append(part.astype(bf16))
        value = value - part
    return parts


def shards(activations, cotangents, left_stats, right_stats, left_roots, right_roots):
    ny = lax.axis_size("y")
    nfar = lax.axis_size("far")
    nnear = lax.axis_size("near")
    nz = nfar * nnear
    tensors = lax.axis_size("tensor")
    y = lax.axis_index("y")
    z = lax.axis_index(Z)
    features = activations.shape[1]
    width = cotangents.shape[1]
    blocks = features // BLOCK
    mine = left_roots.shape[2]
    root_rows = mine * (BLOCK // width)

    partial = lax.dot_general(
        activations, cotangents, (((0,), (0,)), ((), ())), preferred_element_type=f32
    ).reshape(blocks, BLOCK, width)
    roots = left_roots[0].astype(bf16).reshape(blocks, root_rows, width)
    got = swap(jnp.concatenate([partial.astype(bf16), roots], axis=1), "y")
    roots = got[:, BLOCK:].reshape(ny * mine, BLOCK)
    kept = lax.dynamic_index_in_dim(partial, y, 0, keepdims=False)
    others = jnp.where((jnp.arange(ny) == y)[:, None, None], 0.0, got[:, :BLOCK].astype(f32))
    column_part = kept + jnp.sum(others, axis=0)

    got = swap(column_part.astype(bf16).reshape(nnear, BLOCK // nnear, width), "near")
    part = jnp.sum(got.astype(f32), axis=0).astype(bf16)
    part, roots = lax.optimization_barrier((part, roots))
    roots = lax.all_gather(roots, "far", axis=0, tiled=True)
    got, roots = lax.optimization_barrier((everyone(part, "far"), roots))
    own = jnp.sum(got.astype(f32), axis=0).astype(bf16)
    gradient = everyone(own, "near").reshape(BLOCK, width)

    inner = lax.dot_general(
        gradient, gradient, (((0,), (0,)), ((), ())), preferred_element_type=f32
    )
    wide = gradient.astype(f32)
    grad_sq = jnp.sum(wide * wide, axis=0)
    block_sq = lax.psum(grad_sq, "tensor")

    right = lax.dynamic_index_in_dim(right_roots[0], y, 0, keepdims=False)
    mixed = jnp.dot(roots, gradient, preferred_element_type=f32)
    direction = jnp.dot(mixed, right, precision=highest).astype(bf16)
    direction = everyone(direction, "near").reshape(nnear, nfar, ny, mine, width)
    direction = direction.transpose(2, 1, 0, 3, 4).reshape(BLOCK, width)
    wide = direction.astype(f32)
    dir_sq = jnp.sum(wide * wide, axis=0)

    rows = lax.dynamic_index_in_dim(gradient.reshape(ny, nz, mine, width), z, 1, keepdims=False)
    outer = lax.dot_general(
        rows.reshape(ny * mine, width), gradient, (((1,), (1,)), ((), ())), preferred_element_type=f32
    )
    outer = outer.astype(bf16).reshape(ny, root_rows, width)
    inner = lax.dynamic_index_in_dim(inner.reshape(ny, nz, width), z, 1, keepdims=True).astype(bf16)
    line = jnp.arange(16)[:, None]
    extra = jnp.broadcast_to(inner, (ny, 16, width))
    for place, values in enumerate(thirds(grad_sq) + thirds(dir_sq) + thirds(block_sq), 1):
        extra = jnp.where(line == place, values, extra)
    got = swap(
        jnp.concatenate(
            [jnp.broadcast_to(direction[None], (ny, BLOCK, width)), outer, extra], axis=1
        ),
        "y",
    )
    extra = got[:, BLOCK + root_rows :].astype(f32)
    grad_sq, dir_sq, block_sq = (
        jnp.sum(extra[:, 1 + 3 * n : 4 + 3 * n], axis=(1, 2), keepdims=True) for n in range(3)
    )
    layer_sq = jnp.sum(block_sq, axis=0, keepdims=True)
    factor = jnp.sqrt(grad_sq / dir_sq) / jnp.sqrt(layer_sq / (features * width * tensors))
    update = (got[:, :BLOCK].astype(f32) * factor).astype(bf16)
    update = update.reshape(blocks * BLOCK, width)
    outer = got[:, BLOCK : BLOCK + root_rows].astype(f32).reshape(blocks, mine, BLOCK)
    left_new = stat_decay * left_stats + ((1.0 - stat_decay) / width) * outer[None]
    right_new = stat_decay * right_stats + ((1.0 - stat_decay) / BLOCK) * extra[None, :, :1]
    return (update, left_new, right_new)


def solution(mesh):
    dp, tensor = mesh.devices.shape
    blocks, near = 4, 8
    fine = Mesh(
        mesh.devices.reshape(blocks, dp // (blocks * near), near, tensor),
        ("y", "far", "near", "tensor"),
    )
    dp = ("y", *Z)
    in_specs = (
        P(dp, None),
        P(dp, "tensor"),
        P("tensor", None, dp, None),
        P("tensor", None, dp, None),
        P("tensor", None, dp, None),
        P("tensor", None, None, None),
    )
    out_specs = (P(None, "tensor"), P("tensor", None, dp, None), P("tensor", None, dp, None))
    return jax.shard_map(shards, mesh=fine, in_specs=in_specs, out_specs=out_specs, check_vma=False)
```

```python
import jax
import jax.numpy as jnp
from jax import lax
from jax.sharding import Mesh, PartitionSpec as P

BLOCK = 1024
stat_decay = 0.95
highest = lax.Precision.HIGHEST
f32 = jnp.float32
bf16 = jnp.bfloat16
Z = ("far", "near")


def swap(pieces, axis):
    return lax.all_to_all(pieces, axis, 0, 0, tiled=True)


def everyone(piece, axis):
    return swap(jnp.broadcast_to(piece[None], (lax.axis_size(axis), *piece.shape)), axis)


def thirds(value):
    parts = []
    for _ in range(3):
        part = lax.reduce_precision(value, 8, 7)
        parts.append(part.astype(bf16))
        value = value - part
    return parts


def lines(block, values):
    row = jnp.arange(block.shape[-2])[:, None]
    for place, value in enumerate(values, 1):
        block = jnp.where(row == place, value, block)
    return block


def shards(activations, cotangents, left_stats, right_stats, left_roots, right_roots):
    ny = lax.axis_size("y")
    nfar = lax.axis_size("far")
    nnear = lax.axis_size("near")
    nz = nfar * nnear
    tensors = lax.axis_size("tensor")
    y = lax.axis_index("y")
    z = lax.axis_index(Z)
    features = activations.shape[1]
    width = cotangents.shape[1]
    blocks = features // BLOCK
    mine = left_roots.shape[2]
    root_rows = mine * (BLOCK // width)

    partial = lax.dot_general(
        activations, cotangents, (((0,), (0,)), ((), ())), preferred_element_type=f32
    ).reshape(blocks, BLOCK, width)
    roots = left_roots[0].astype(bf16).reshape(blocks, root_rows, width)
    got = swap(jnp.concatenate([partial.astype(bf16), roots], axis=1), "y")
    roots = got[:, BLOCK:].reshape(ny * mine, BLOCK)
    kept = lax.dynamic_index_in_dim(partial, y, 0, keepdims=False)
    others = jnp.where((jnp.arange(ny) == y)[:, None, None], 0.0, got[:, :BLOCK].astype(f32))
    column_part = kept + jnp.sum(others, axis=0)

    pieces = column_part.astype(bf16).reshape(nnear, BLOCK // nnear, width)
    pieces, roots = lax.optimization_barrier((pieces, roots))
    roots = lax.all_gather(roots, "far", axis=0, tiled=True)
    got, roots = lax.optimization_barrier((swap(pieces, "near"), roots))
    part = jnp.sum(got.astype(f32), axis=0).astype(bf16)
    got = everyone(part, "far")
    own = jnp.sum(got.astype(f32), axis=0)
    own_sq = lax.psum(jnp.sum(own * own, axis=0), "tensor")
    own = own.astype(bf16)
    gradient, own_sq = lax.optimization_barrier((everyone(own, "near"), own_sq))
    gradient = gradient.reshape(BLOCK, width)

    inner = lax.dot_general(
        gradient, gradient, (((0,), (0,)), ((), ())), preferred_element_type=f32
    )
    wide = gradient.astype(f32)
    grad_sq = jnp.sum(wide * wide, axis=0)

    right = lax.dynamic_index_in_dim(right_roots[0], y, 0, keepdims=False)
    mixed = jnp.dot(roots, gradient, preferred_element_type=f32)
    direction = jnp.dot(mixed, right, precision=highest).astype(bf16)
    got = everyone(
        jnp.concatenate([direction, lines(jnp.zeros((16, width), bf16), thirds(own_sq))], axis=0), "near"
    )
    block_sq = jnp.sum(got[:, nfar * ny * mine :].astype(f32), axis=(0, 1))
    direction = got[:, : nfar * ny * mine].reshape(nnear, nfar, ny, mine, width)
    direction = direction.transpose(2, 1, 0, 3, 4).reshape(BLOCK, width)
    wide = direction.astype(f32)
    dir_sq = jnp.sum(wide * wide, axis=0)

    rows = lax.dynamic_index_in_dim(gradient.reshape(ny, nz, mine, width), z, 1, keepdims=False)
    outer = lax.dot_general(
        rows.reshape(ny * mine, width), gradient, (((1,), (1,)), ((), ())), preferred_element_type=f32
    )
    outer = outer.astype(bf16).reshape(ny, root_rows, width)
    inner = lax.dynamic_index_in_dim(inner.reshape(ny, nz, width), z, 1, keepdims=True).astype(bf16)
    extra = lines(
        jnp.broadcast_to(inner, (ny, 16, width)), thirds(grad_sq) + thirds(dir_sq) + thirds(block_sq)
    )
    got = swap(
        jnp.concatenate(
            [jnp.broadcast_to(direction[None], (ny, BLOCK, width)), outer, extra], axis=1
        ),
        "y",
    )
    extra = got[:, BLOCK + root_rows :].astype(f32)
    grad_sq, dir_sq, block_sq = (
        jnp.sum(extra[:, 1 + 3 * n : 4 + 3 * n], axis=(1, 2), keepdims=True) for n in range(3)
    )
    layer_sq = jnp.sum(block_sq, axis=0, keepdims=True)
    factor = jnp.sqrt(grad_sq / dir_sq) / jnp.sqrt(layer_sq / (features * width * tensors))
    update = (got[:, :BLOCK].astype(f32) * factor).astype(bf16)
    update = update.reshape(blocks * BLOCK, width)
    outer = got[:, BLOCK : BLOCK + root_rows].astype(f32).reshape(blocks, mine, BLOCK)
    left_new = stat_decay * left_stats + ((1.0 - stat_decay) / width) * outer[None]
    right_new = stat_decay * right_stats + ((1.0 - stat_decay) / BLOCK) * extra[None, :, :1]
    return (update, left_new, right_new)


def solution(mesh):
    dp, tensor = mesh.devices.shape
    blocks, near = 4, 8
    fine = Mesh(
        mesh.devices.reshape(blocks, dp // (blocks * near), near, tensor),
        ("y", "far", "near", "tensor"),
    )
    dp = ("y", *Z)
    in_specs = (
        P(dp, None),
        P(dp, "tensor"),
        P("tensor", None, dp, None),
        P("tensor", None, dp, None),
        P("tensor", None, dp, None),
        P("tensor", None, None, None),
    )
    out_specs = (P(None, "tensor"), P("tensor", None, dp, None), P("tensor", None, dp, None))
    return jax.shard_map(shards, mesh=fine, in_specs=in_specs, out_specs=out_specs, check_vma=False)
```

```python
import jax
import jax.numpy as jnp
from jax import lax
from jax.sharding import Mesh, PartitionSpec as P

BLOCK = 1024
stat_decay = 0.95
highest = lax.Precision.HIGHEST
f32 = jnp.float32
bf16 = jnp.bfloat16
Z = ("far", "near")


def swap(pieces, axis):
    return lax.all_to_all(pieces, axis, 0, 0, tiled=True)


def everyone(piece, axis):
    return swap(jnp.broadcast_to(piece[None], (lax.axis_size(axis), *piece.shape)), axis)


def thirds(value):
    parts = []
    for _ in range(3):
        part = lax.reduce_precision(value, 8, 7)
        parts.append(part.astype(bf16))
        value = value - part
    return parts


def sum_tokens(rows, columns):
    return lax.dot_general(rows, columns, (((0,), (0,)), ((), ())), preferred_element_type=f32)


def shards(activations, cotangents, left_stats, right_stats, left_roots, right_roots):
    ny = lax.axis_size("y")
    nfar = lax.axis_size("far")
    nnear = lax.axis_size("near")
    nz = nfar * nnear
    tensors = lax.axis_size("tensor")
    y = lax.axis_index("y")
    z = lax.axis_index(Z)
    features = activations.shape[1]
    width = cotangents.shape[1]
    blocks = features // BLOCK
    mine = left_roots.shape[2]
    root_rows = mine * (BLOCK // width)

    partial = sum_tokens(activations, cotangents).astype(bf16).reshape(blocks, BLOCK, width)
    roots = left_roots[0].astype(bf16).reshape(blocks, root_rows, width)
    got = swap(jnp.concatenate([partial, roots], axis=1), "y")
    roots = got[:, BLOCK:].reshape(ny * mine, BLOCK)
    kept = sum_tokens(lax.dynamic_slice_in_dim(activations, y * BLOCK, BLOCK, 1), cotangents)
    others = jnp.where((jnp.arange(ny) == y)[:, None, None], 0.0, got[:, :BLOCK].astype(f32))
    column_part = kept + jnp.sum(others, axis=0)

    pieces = column_part.astype(bf16).reshape(nnear, BLOCK // nnear, width)
    pieces, roots = lax.optimization_barrier((pieces, roots))
    roots = lax.all_gather(roots, "far", axis=0, tiled=True)
    got, roots = lax.optimization_barrier((swap(pieces, "near"), roots))
    part = jnp.sum(got.astype(f32), axis=0).astype(bf16)
    got = everyone(part, "far")
    own = jnp.sum(got.astype(f32), axis=0).astype(bf16)
    gradient = everyone(own, "near").reshape(BLOCK, width)

    inner = lax.dot_general(
        gradient, gradient, (((0,), (0,)), ((), ())), preferred_element_type=f32
    )
    wide = gradient.astype(f32)
    grad_sq = jnp.sum(wide * wide, axis=0)
    block_sq = lax.psum(grad_sq, "tensor")

    right = lax.dynamic_index_in_dim(right_roots[0], y, 0, keepdims=False)
    mixed = jnp.dot(roots, gradient, preferred_element_type=f32)
    direction = jnp.dot(mixed, right, precision=highest).astype(bf16)
    direction = everyone(direction, "near").reshape(nnear, nfar, ny, mine, width)
    direction = direction.transpose(2, 1, 0, 3, 4).reshape(BLOCK, width)
    wide = direction.astype(f32)
    dir_sq = jnp.sum(wide * wide, axis=0)

    rows = lax.dynamic_index_in_dim(gradient.reshape(ny, nz, mine, width), z, 1, keepdims=False)
    outer = lax.dot_general(
        rows.reshape(ny * mine, width), gradient, (((1,), (1,)), ((), ())), preferred_element_type=f32
    )
    outer = outer.astype(bf16).reshape(ny, root_rows, width)
    inner = lax.dynamic_index_in_dim(inner.reshape(ny, nz, width), z, 1, keepdims=True).astype(bf16)
    line = jnp.arange(16)[:, None]
    extra = jnp.broadcast_to(inner, (ny, 16, width))
    for place, values in enumerate(thirds(grad_sq) + thirds(dir_sq) + thirds(block_sq), 1):
        extra = jnp.where(line == place, values, extra)
    got = swap(
        jnp.concatenate(
            [jnp.broadcast_to(direction[None], (ny, BLOCK, width)), outer, extra], axis=1
        ),
        "y",
    )
    extra = got[:, BLOCK + root_rows :].astype(f32)
    grad_sq, dir_sq, block_sq = (
        jnp.sum(extra[:, 1 + 3 * n : 4 + 3 * n], axis=(1, 2), keepdims=True) for n in range(3)
    )
    layer_sq = jnp.sum(block_sq, axis=0, keepdims=True)
    factor = jnp.sqrt(grad_sq / dir_sq) / jnp.sqrt(layer_sq / (features * width * tensors))
    update = (got[:, :BLOCK].astype(f32) * factor).astype(bf16)
    update = update.reshape(blocks * BLOCK, width)
    outer = got[:, BLOCK : BLOCK + root_rows].astype(f32).reshape(blocks, mine, BLOCK)
    left_new = stat_decay * left_stats + ((1.0 - stat_decay) / width) * outer[None]
    right_new = stat_decay * right_stats + ((1.0 - stat_decay) / BLOCK) * extra[None, :, :1]
    return (update, left_new, right_new)


def solution(mesh):
    dp, tensor = mesh.devices.shape
    blocks, near = 4, 8
    fine = Mesh(
        mesh.devices.reshape(blocks, dp // (blocks * near), near, tensor),
        ("y", "far", "near", "tensor"),
    )
    dp = ("y", *Z)
    in_specs = (
        P(dp, None),
        P(dp, "tensor"),
        P("tensor", None, dp, None),
        P("tensor", None, dp, None),
        P("tensor", None, dp, None),
        P("tensor", None, None, None),
    )
    out_specs = (P(None, "tensor"), P("tensor", None, dp, None), P("tensor", None, dp, None))
    return jax.shard_map(shards, mesh=fine, in_specs=in_specs, out_specs=out_specs, check_vma=False)
```

```python
import jax
import jax.numpy as jnp
from jax import lax
from jax.sharding import Mesh, PartitionSpec as P

BLOCK = 1024
stat_decay = 0.95
highest = lax.Precision.HIGHEST
f32 = jnp.float32
bf16 = jnp.bfloat16
Z = ("far", "mid", "pair")


def swap(pieces, axis):
    return lax.all_to_all(pieces, axis, 0, 0, tiled=True)


def everyone(piece, axis):
    return swap(jnp.broadcast_to(piece[None], (lax.axis_size(axis), *piece.shape)), axis)


def thirds(value):
    parts = []
    for _ in range(3):
        part = lax.reduce_precision(value, 8, 7)
        parts.append(part.astype(bf16))
        value = value - part
    return parts


def sum_tokens(rows, columns):
    return lax.dot_general(rows, columns, (((0,), (0,)), ((), ())), preferred_element_type=f32)


def shards(activations, cotangents, left_stats, right_stats, left_roots, right_roots):
    ny = lax.axis_size("y")
    nfar = lax.axis_size("far")
    nmid = lax.axis_size("mid")
    npair = lax.axis_size("pair")
    nz = nfar * nmid * npair
    tensors = lax.axis_size("tensor")
    y = lax.axis_index("y")
    pair = lax.axis_index("pair")
    place = y * npair + pair
    features = activations.shape[1]
    width = cotangents.shape[1]
    blocks = features // BLOCK
    mine = left_roots.shape[2]
    root_rows = mine * (BLOCK // width)

    half = BLOCK // npair
    partial = sum_tokens(activations, cotangents).astype(bf16)
    partial = partial.reshape(blocks * npair, half, width)
    roots = left_roots[0].astype(bf16).reshape(blocks, 1, root_rows, width)
    roots = jnp.broadcast_to(roots, (blocks, npair, root_rows, width))
    roots = roots.reshape(blocks * npair, root_rows, width)
    got = swap(jnp.concatenate([partial, roots], axis=1), ("y", "pair"))
    roots = got[:, half:].reshape(ny, npair, root_rows, width)
    roots = lax.dynamic_index_in_dim(roots, pair, 1, keepdims=False).reshape(ny * mine, BLOCK)
    kept = sum_tokens(lax.dynamic_slice_in_dim(activations, place * half, half, 1), cotangents)
    others = jnp.arange(ny * npair) == place
    others = jnp.where(others[:, None, None], 0.0, got[:, :half].astype(f32))
    column_part = kept + jnp.sum(others, axis=0)

    pieces = column_part.astype(bf16).reshape(nmid, half // nmid, width)
    pieces, roots = lax.optimization_barrier((pieces, roots))
    roots = lax.all_gather(roots, "far", axis=0, tiled=True)
    got, roots = lax.optimization_barrier((swap(pieces, "mid"), roots))
    part = jnp.sum(got.astype(f32), axis=0).astype(bf16)
    got = everyone(part, "far")
    own = jnp.sum(got.astype(f32), axis=0).astype(bf16)
    gradient = everyone(own, ("pair", "mid")).reshape(BLOCK, width)

    inner = lax.dot_general(
        gradient, gradient, (((0,), (0,)), ((), ())), preferred_element_type=f32
    )
    wide = gradient.astype(f32)
    grad_sq = jnp.sum(wide * wide, axis=0)
    block_sq = lax.psum(grad_sq, "tensor")

    right = lax.dynamic_index_in_dim(right_roots[0], y, 0, keepdims=False)
    mixed = jnp.dot(roots, gradient, preferred_element_type=f32)
    direction = jnp.dot(mixed, right, precision=highest).astype(bf16)
    direction = everyone(direction, "mid").reshape(nmid, nfar, ny, mine, width)
    direction = direction.transpose(2, 1, 0, 3, 4).reshape(half, width)
    wide = direction.astype(f32)
    dir_sq = jnp.sum(wide * wide, axis=0)

    spot = lax.axis_index("far") * nmid + lax.axis_index("mid")
    rows = gradient.reshape(ny, nz // npair, npair * mine, width)
    rows = lax.dynamic_index_in_dim(rows, spot, 1, keepdims=False).reshape(ny * npair * mine, width)
    outer = lax.dot_general(
        rows,
        lax.dynamic_slice_in_dim(gradient, pair * half, half, 0),
        (((1,), (1,)), ((), ())),
        preferred_element_type=f32,
    )
    outer_rows = root_rows // npair
    outer = outer.astype(bf16).reshape(ny * npair, outer_rows, width)
    inner = inner.reshape(ny, nz // npair, npair, width)
    inner = lax.dynamic_index_in_dim(inner, spot, 1, keepdims=False).astype(bf16)
    inner = inner.reshape(ny * npair, 1, width)
    line = jnp.arange(16)[:, None]
    extra = jnp.broadcast_to(inner, (ny * npair, 16, width))
    for number, values in enumerate(thirds(grad_sq) + thirds(dir_sq) + thirds(block_sq), 1):
        extra = jnp.where(line == number, values, extra)
    got = swap(
        jnp.concatenate(
            [jnp.broadcast_to(direction[None], (ny * npair, half, width)), outer, extra], axis=1
        ),
        ("y", "pair"),
    )
    got = got.reshape(blocks, npair, half + outer_rows + 16, width)
    extra = got[:, :, half + outer_rows :].astype(f32)
    grad_sq = jnp.sum(extra[:, :1, 1:4], axis=(1, 2, 3), keepdims=True)
    dir_sq = jnp.sum(extra[:, :, 4:7], axis=(1, 2, 3), keepdims=True)
    layer_sq = jnp.sum(extra[:, :1, 7:10], keepdims=True)
    factor = jnp.sqrt(grad_sq / dir_sq) / jnp.sqrt(layer_sq / (features * width * tensors))
    update = (got[:, :, :half].astype(f32) * factor).astype(bf16)
    update = update.reshape(blocks, npair, half // mine, mine, width).transpose(0, 2, 1, 3, 4)
    update = update.reshape(blocks * BLOCK, width)
    outer = got[:, :, half : half + outer_rows].astype(f32)
    outer = outer.reshape(blocks, npair, mine, half).transpose(0, 2, 1, 3)
    outer = outer.reshape(blocks, mine, BLOCK)
    left_new = stat_decay * left_stats + ((1.0 - stat_decay) / width) * outer[None]
    right_new = stat_decay * right_stats + ((1.0 - stat_decay) / BLOCK) * extra[None, :, 0, :1]
    return (update, left_new, right_new)


def solution(mesh):
    dp, tensor = mesh.devices.shape
    blocks, mid, pair = 4, 4, 2
    fine = Mesh(
        mesh.devices.reshape(blocks, dp // (blocks * mid * pair), mid, pair, tensor),
        ("y", "far", "mid", "pair", "tensor"),
    )
    dp = ("y", *Z)
    in_specs = (
        P(dp, None),
        P(dp, "tensor"),
        P("tensor", None, dp, None),
        P("tensor", None, dp, None),
        P("tensor", None, dp, None),
        P("tensor", None, None, None),
    )
    out_specs = (P(None, "tensor"), P("tensor", None, dp, None), P("tensor", None, dp, None))
    return jax.shard_map(shards, mesh=fine, in_specs=in_specs, out_specs=out_specs, check_vma=False)
```

```python
import jax
import jax.numpy as jnp
from jax import lax
from jax.sharding import Mesh, PartitionSpec as P

BLOCK = 1024
stat_decay = 0.95
highest = lax.Precision.HIGHEST
f32 = jnp.float32
bf16 = jnp.bfloat16
Z = ("far", "mid", "pair")


def swap(pieces, axis):
    return lax.all_to_all(pieces, axis, 0, 0, tiled=True)


def everyone(piece, axis):
    return swap(jnp.broadcast_to(piece[None], (lax.axis_size(axis), *piece.shape)), axis)


def thirds(value):
    parts = []
    for _ in range(3):
        part = lax.reduce_precision(value, 8, 7)
        parts.append(part.astype(bf16))
        value = value - part
    return parts


def sum_tokens(rows, columns):
    return lax.dot_general(rows, columns, (((0,), (0,)), ((), ())), preferred_element_type=f32)


def shards(activations, cotangents, left_stats, right_stats, left_roots, right_roots):
    ny = lax.axis_size("y")
    nfar = lax.axis_size("far")
    nmid = lax.axis_size("mid")
    npair = lax.axis_size("pair")
    nz = nfar * nmid * npair
    tensors = lax.axis_size("tensor")
    y = lax.axis_index("y")
    z = lax.axis_index(Z)
    pair = lax.axis_index("pair")
    place = y * npair + pair
    features = activations.shape[1]
    width = cotangents.shape[1]
    blocks = features // BLOCK
    mine = left_roots.shape[2]
    root_rows = mine * (BLOCK // width)

    half = BLOCK // npair
    partial = sum_tokens(activations, cotangents).astype(bf16)
    partial = partial.reshape(blocks * npair, half, width)
    roots = left_roots[0].astype(bf16).reshape(blocks, 1, root_rows, width)
    roots = jnp.broadcast_to(roots, (blocks, npair, root_rows, width))
    roots = roots.reshape(blocks * npair, root_rows, width)
    got = swap(jnp.concatenate([partial, roots], axis=1), ("y", "pair"))
    roots = got[:, half:].reshape(ny, npair, root_rows, width)
    roots = lax.dynamic_index_in_dim(roots, pair, 1, keepdims=False).reshape(ny * mine, BLOCK)
    kept = sum_tokens(lax.dynamic_slice_in_dim(activations, place * half, half, 1), cotangents)
    others = jnp.arange(ny * npair) == place
    others = jnp.where(others[:, None, None], 0.0, got[:, :half].astype(f32))
    column_part = kept + jnp.sum(others, axis=0)

    pieces = column_part.astype(bf16).reshape(nmid, half // nmid, width)
    pieces, roots = lax.optimization_barrier((pieces, roots))
    roots = lax.all_gather(roots, "far", axis=0, tiled=True)
    got, roots = lax.optimization_barrier((swap(pieces, "mid"), roots))
    part = jnp.sum(got.astype(f32), axis=0).astype(bf16)
    got = everyone(part, "far")
    own = jnp.sum(got.astype(f32), axis=0).astype(bf16)
    gradient = everyone(own, ("pair", "mid")).reshape(BLOCK, width)

    inner = lax.dot_general(
        gradient, gradient, (((0,), (0,)), ((), ())), preferred_element_type=f32
    )
    wide = gradient.astype(f32)
    grad_sq = jnp.sum(wide * wide, axis=0)
    block_sq = lax.psum(grad_sq, "tensor")

    right = lax.dynamic_index_in_dim(right_roots[0], y, 0, keepdims=False)
    mixed = jnp.dot(roots, gradient, preferred_element_type=f32)
    direction = jnp.dot(mixed, right, precision=highest).astype(bf16)
    direction = everyone(direction, ("mid", "pair")).reshape(nmid * npair, nfar, ny, mine, width)
    direction = direction.transpose(2, 1, 0, 3, 4).reshape(BLOCK, width)
    wide = direction.astype(f32)
    dir_sq = jnp.sum(wide * wide, axis=0)

    rows = lax.dynamic_index_in_dim(gradient.reshape(ny, nz, mine, width), z, 1, keepdims=False)
    outer = lax.dot_general(
        rows.reshape(ny * mine, width), gradient, (((1,), (1,)), ((), ())), preferred_element_type=f32
    )
    outer = outer.astype(bf16).reshape(ny, root_rows, width)
    inner = lax.dynamic_index_in_dim(inner.reshape(ny, nz, width), z, 1, keepdims=True).astype(bf16)
    line = jnp.arange(16)[:, None]
    extra = jnp.broadcast_to(inner, (ny, 16, width))
    for place, values in enumerate(thirds(grad_sq) + thirds(dir_sq) + thirds(block_sq), 1):
        extra = jnp.where(line == place, values, extra)
    got = swap(
        jnp.concatenate(
            [jnp.broadcast_to(direction[None], (ny, BLOCK, width)), outer, extra], axis=1
        ),
        "y",
    )
    extra = got[:, BLOCK + root_rows :].astype(f32)
    grad_sq, dir_sq, block_sq = (
        jnp.sum(extra[:, 1 + 3 * n : 4 + 3 * n], axis=(1, 2), keepdims=True) for n in range(3)
    )
    layer_sq = jnp.sum(block_sq, axis=0, keepdims=True)
    factor = jnp.sqrt(grad_sq / dir_sq) / jnp.sqrt(layer_sq / (features * width * tensors))
    update = (got[:, :BLOCK].astype(f32) * factor).astype(bf16)
    update = update.reshape(blocks * BLOCK, width)
    outer = got[:, BLOCK : BLOCK + root_rows].astype(f32).reshape(blocks, mine, BLOCK)
    left_new = stat_decay * left_stats + ((1.0 - stat_decay) / width) * outer[None]
    right_new = stat_decay * right_stats + ((1.0 - stat_decay) / BLOCK) * extra[None, :, :1]
    return (update, left_new, right_new)


def solution(mesh):
    dp, tensor = mesh.devices.shape
    blocks, mid, pair = 4, 4, 2
    fine = Mesh(
        mesh.devices.reshape(blocks, dp // (blocks * mid * pair), mid, pair, tensor),
        ("y", "far", "mid", "pair", "tensor"),
    )
    dp = ("y", *Z)
    in_specs = (
        P(dp, None),
        P(dp, "tensor"),
        P("tensor", None, dp, None),
        P("tensor", None, dp, None),
        P("tensor", None, dp, None),
        P("tensor", None, None, None),
    )
    out_specs = (P(None, "tensor"), P("tensor", None, dp, None), P("tensor", None, dp, None))
    return jax.shard_map(shards, mesh=fine, in_specs=in_specs, out_specs=out_specs, check_vma=False)
```

```python
import jax
import jax.numpy as jnp
from jax import lax
from jax.sharding import Mesh, PartitionSpec as P

BLOCK = 1024
stat_decay = 0.95
highest = lax.Precision.HIGHEST
f32 = jnp.float32
bf16 = jnp.bfloat16
Z = ("far", "mid", "pair")


def swap(pieces, axis):
    return lax.all_to_all(pieces, axis, 0, 0, tiled=True)


def everyone(piece, axis):
    return swap(jnp.broadcast_to(piece[None], (lax.axis_size(axis), *piece.shape)), axis)


def thirds(value):
    parts = []
    for _ in range(3):
        part = lax.reduce_precision(value, 8, 7)
        parts.append(part.astype(bf16))
        value = value - part
    return parts


def sum_tokens(rows, columns):
    return lax.dot_general(rows, columns, (((0,), (0,)), ((), ())), preferred_element_type=f32)


def shards(activations, cotangents, left_stats, right_stats, left_roots, right_roots):
    ny = lax.axis_size("y")
    nfar = lax.axis_size("far")
    nmid = lax.axis_size("mid")
    npair = lax.axis_size("pair")
    nz = nfar * nmid * npair
    tensors = lax.axis_size("tensor")
    y = lax.axis_index("y")
    z = lax.axis_index(Z)
    pair = lax.axis_index("pair")
    place = y * npair + pair
    features = activations.shape[1]
    width = cotangents.shape[1]
    blocks = features // BLOCK
    mine = left_roots.shape[2]
    root_rows = mine * (BLOCK // width)

    half = BLOCK // npair
    partial = sum_tokens(activations, cotangents).astype(bf16)
    partial = partial.reshape(blocks * npair, half, width)
    partial, roots = lax.optimization_barrier((partial, left_roots[0].astype(bf16)))
    roots = lax.all_gather(roots, "far")
    got, roots = lax.optimization_barrier((swap(partial, ("y", "pair")), roots))
    kept = sum_tokens(lax.dynamic_slice_in_dim(activations, place * half, half, 1), cotangents)
    others = jnp.arange(ny * npair) == place
    others = jnp.where(others[:, None, None], 0.0, got.astype(f32))
    column_part = kept + jnp.sum(others, axis=0)

    got = swap(column_part.astype(bf16).reshape(nmid, half // nmid, width), "mid")
    part = jnp.sum(got.astype(f32), axis=0).astype(bf16)
    part, roots = lax.optimization_barrier((part, roots))
    held = [lax.dynamic_index_in_dim(roots, y, 1, keepdims=False)]
    for step in range(1, ny):
        turn = [(i, (i - step) % ny) for i in range(ny)]
        block = lax.dynamic_index_in_dim(roots, (y - step) % ny, 1, keepdims=False)
        held.append(lax.ppermute(block, "y", turn))
    roots = lax.dynamic_slice_in_dim(jnp.stack(held + held), (ny - y) % ny, ny, 0)
    roots = roots.reshape(ny * nfar * mine, BLOCK)
    got, roots = lax.optimization_barrier((everyone(part, "far"), roots))
    own = jnp.sum(got.astype(f32), axis=0).astype(bf16)
    gradient = everyone(own, ("pair", "mid")).reshape(BLOCK, width)

    inner = lax.dot_general(
        gradient, gradient, (((0,), (0,)), ((), ())), preferred_element_type=f32
    )
    wide = gradient.astype(f32)
    grad_sq = jnp.sum(wide * wide, axis=0)
    block_sq = jnp.sum(lax.all_gather(grad_sq, "tensor"), axis=0)

    right = lax.dynamic_index_in_dim(right_roots[0], y, 0, keepdims=False)
    mixed = jnp.dot(roots, gradient, preferred_element_type=f32)
    direction = jnp.dot(mixed, right, precision=highest).astype(bf16)
    direction = everyone(direction, ("mid", "pair")).reshape(nmid * npair, ny, nfar, mine, width)
    direction = direction.transpose(1, 2, 0, 3, 4).reshape(BLOCK, width)
    wide = direction.astype(f32)
    dir_sq = jnp.sum(wide * wide, axis=0)

    rows = lax.dynamic_index_in_dim(gradient.reshape(ny, nz, mine, width), z, 1, keepdims=False)
    outer = lax.dot_general(
        rows.reshape(ny * mine, width), gradient, (((1,), (1,)), ((), ())), preferred_element_type=f32
    )
    outer = outer.astype(bf16).reshape(ny, root_rows, width)
    inner = lax.dynamic_index_in_dim(inner.reshape(ny, nz, width), z, 1, keepdims=True).astype(bf16)
    line = jnp.arange(16)[:, None]
    extra = jnp.broadcast_to(inner, (ny, 16, width))
    for place, values in enumerate(thirds(grad_sq) + thirds(dir_sq) + thirds(block_sq), 1):
        extra = jnp.where(line == place, values, extra)
    got = swap(
        jnp.concatenate(
            [jnp.broadcast_to(direction[None], (ny, BLOCK, width)), outer, extra], axis=1
        ),
        "y",
    )
    extra = got[:, BLOCK + root_rows :].astype(f32)
    grad_sq, dir_sq, block_sq = (
        jnp.sum(extra[:, 1 + 3 * n : 4 + 3 * n], axis=(1, 2), keepdims=True) for n in range(3)
    )
    layer_sq = jnp.sum(block_sq, axis=0, keepdims=True)
    factor = jnp.sqrt(grad_sq / dir_sq) / jnp.sqrt(layer_sq / (features * width * tensors))
    update = (got[:, :BLOCK].astype(f32) * factor).astype(bf16)
    update = update.reshape(blocks * BLOCK, width)
    outer = got[:, BLOCK : BLOCK + root_rows].astype(f32).reshape(blocks, mine, BLOCK)
    left_new = stat_decay * left_stats + ((1.0 - stat_decay) / width) * outer[None]
    right_new = stat_decay * right_stats + ((1.0 - stat_decay) / BLOCK) * extra[None, :, :1]
    return (update, left_new, right_new)


def solution(mesh):
    dp, tensor = mesh.devices.shape
    blocks, mid, pair = 4, 4, 2
    fine = Mesh(
        mesh.devices.reshape(blocks, dp // (blocks * mid * pair), mid, pair, tensor),
        ("y", "far", "mid", "pair", "tensor"),
    )
    dp = ("y", *Z)
    in_specs = (
        P(dp, None),
        P(dp, "tensor"),
        P("tensor", None, dp, None),
        P("tensor", None, dp, None),
        P("tensor", None, dp, None),
        P("tensor", None, None, None),
    )
    out_specs = (P(None, "tensor"), P("tensor", None, dp, None), P("tensor", None, dp, None))
    return jax.shard_map(shards, mesh=fine, in_specs=in_specs, out_specs=out_specs, check_vma=False)
```

```python
import jax
import jax.numpy as jnp
from jax import lax
from jax.sharding import Mesh, PartitionSpec as P

BLOCK = 1024
stat_decay = 0.95
highest = lax.Precision.HIGHEST
f32 = jnp.float32
bf16 = jnp.bfloat16
Z = ("far", "near")


def swap(pieces, axis):
    return lax.all_to_all(pieces, axis, 0, 0, tiled=True)


def everyone(piece, axis):
    return swap(jnp.broadcast_to(piece[None], (lax.axis_size(axis), *piece.shape)), axis)


def thirds(value):
    parts = []
    for _ in range(3):
        part = lax.reduce_precision(value, 8, 7)
        parts.append(part.astype(bf16))
        value = value - part
    return parts


def sum_tokens(rows, columns):
    return lax.dot_general(rows, columns, (((0,), (0,)), ((), ())), preferred_element_type=f32)


def shards(activations, cotangents, left_stats, right_stats, left_roots, right_roots):
    ny = lax.axis_size("y")
    nfar = lax.axis_size("far")
    nnear = lax.axis_size("near")
    nz = nfar * nnear
    tensors = lax.axis_size("tensor")
    y = lax.axis_index("y")
    z = lax.axis_index(Z)
    features = activations.shape[1]
    width = cotangents.shape[1]
    blocks = features // BLOCK
    mine = left_roots.shape[2]
    root_rows = mine * (BLOCK // width)

    partial = sum_tokens(activations, cotangents).astype(bf16).reshape(blocks, BLOCK, width)
    partial, roots = lax.optimization_barrier((partial, left_roots[0].astype(bf16)))
    roots = lax.all_gather(roots, "far")
    got, roots = lax.optimization_barrier((swap(partial, "y"), roots))
    kept = sum_tokens(lax.dynamic_slice_in_dim(activations, y * BLOCK, BLOCK, 1), cotangents)
    others = jnp.where((jnp.arange(ny) == y)[:, None, None], 0.0, got.astype(f32))
    column_part = kept + jnp.sum(others, axis=0)

    got = swap(column_part.astype(bf16).reshape(nnear, BLOCK // nnear, width), "near")
    part = jnp.sum(got.astype(f32), axis=0).astype(bf16)
    part, roots = lax.optimization_barrier((part, roots))
    held = [lax.dynamic_index_in_dim(roots, y, 1, keepdims=False)]
    for step in range(1, ny):
        turn = [(i, (i - step) % ny) for i in range(ny)]
        block = lax.dynamic_index_in_dim(roots, (y - step) % ny, 1, keepdims=False)
        held.append(lax.ppermute(block, "y", turn))
    roots = lax.dynamic_slice_in_dim(jnp.stack(held + held), (ny - y) % ny, ny, 0)
    roots = roots.reshape(ny * nfar * mine, BLOCK)
    got, roots = lax.optimization_barrier((everyone(part, "far"), roots))
    own = jnp.sum(got.astype(f32), axis=0).astype(bf16)
    gradient = everyone(own, "near").reshape(BLOCK, width)

    inner = lax.dot_general(
        gradient, gradient, (((0,), (0,)), ((), ())), preferred_element_type=f32
    )
    wide = gradient.astype(f32)
    grad_sq = jnp.sum(wide * wide, axis=0)
    block_sq = jnp.sum(lax.all_gather(grad_sq, "tensor"), axis=0)

    right = lax.dynamic_index_in_dim(right_roots[0], y, 0, keepdims=False)
    mixed = jnp.dot(roots, gradient, preferred_element_type=f32)
    direction = jnp.dot(mixed, right, precision=highest).astype(bf16)
    direction = everyone(direction, "near").reshape(nnear, ny, nfar, mine, width)
    direction = direction.transpose(1, 2, 0, 3, 4).reshape(BLOCK, width)
    wide = direction.astype(f32)
    dir_sq = jnp.sum(wide * wide, axis=0)

    rows = lax.dynamic_index_in_dim(gradient.reshape(ny, nz, mine, width), z, 1, keepdims=False)
    outer = lax.dot_general(
        rows.reshape(ny * mine, width), gradient, (((1,), (1,)), ((), ())), preferred_element_type=f32
    )
    outer = outer.astype(bf16).reshape(ny, root_rows, width)
    inner = lax.dynamic_index_in_dim(inner.reshape(ny, nz, width), z, 1, keepdims=True).astype(bf16)
    line = jnp.arange(16)[:, None]
    extra = jnp.broadcast_to(inner, (ny, 16, width))
    for place, values in enumerate(thirds(grad_sq) + thirds(dir_sq) + thirds(block_sq), 1):
        extra = jnp.where(line == place, values, extra)
    got = swap(
        jnp.concatenate(
            [jnp.broadcast_to(direction[None], (ny, BLOCK, width)), outer, extra], axis=1
        ),
        "y",
    )
    extra = got[:, BLOCK + root_rows :].astype(f32)
    grad_sq, dir_sq, block_sq = (
        jnp.sum(extra[:, 1 + 3 * n : 4 + 3 * n], axis=(1, 2), keepdims=True) for n in range(3)
    )
    layer_sq = jnp.sum(block_sq, axis=0, keepdims=True)
    factor = jnp.sqrt(grad_sq / dir_sq) / jnp.sqrt(layer_sq / (features * width * tensors))
    update = (got[:, :BLOCK].astype(f32) * factor).astype(bf16)
    update = update.reshape(blocks * BLOCK, width)
    outer = got[:, BLOCK : BLOCK + root_rows].astype(f32).reshape(blocks, mine, BLOCK)
    left_new = stat_decay * left_stats + ((1.0 - stat_decay) / width) * outer[None]
    right_new = stat_decay * right_stats + ((1.0 - stat_decay) / BLOCK) * extra[None, :, :1]
    return (update, left_new, right_new)


def solution(mesh):
    dp, tensor = mesh.devices.shape
    blocks, near = 4, 8
    fine = Mesh(
        mesh.devices.reshape(blocks, dp // (blocks * near), near, tensor),
        ("y", "far", "near", "tensor"),
    )
    dp = ("y", *Z)
    in_specs = (
        P(dp, None),
        P(dp, "tensor"),
        P("tensor", None, dp, None),
        P("tensor", None, dp, None),
        P("tensor", None, dp, None),
        P("tensor", None, None, None),
    )
    out_specs = (P(None, "tensor"), P("tensor", None, dp, None), P("tensor", None, dp, None))
    return jax.shard_map(shards, mesh=fine, in_specs=in_specs, out_specs=out_specs, check_vma=False)
```

```python
import jax
import jax.numpy as jnp
from jax import lax
from jax.experimental import pallas as pl
from jax.experimental.pallas import tpu as pltpu
from jax.sharding import Mesh, PartitionSpec as P

BLOCK = 1024
stat_decay = 0.95
highest = lax.Precision.HIGHEST
f32 = jnp.float32
bf16 = jnp.bfloat16
Z = ("far", "mid", "pair")


def swap(pieces, axis):
    return lax.all_to_all(pieces, axis, 0, 0, tiled=True)


def everyone(piece, axis):
    return swap(jnp.broadcast_to(piece[None], (lax.axis_size(axis), *piece.shape)), axis)


def thirds(value):
    parts = []
    for _ in range(3):
        part = lax.reduce_precision(value, 8, 7)
        parts.append(part.astype(bf16))
        value = value - part
    return parts


def sum_tokens(rows, columns):
    return lax.dot_general(rows, columns, (((0,), (0,)), ((), ())), preferred_element_type=f32)


def finish_kernel(size, got, extras, left_stats, right_stats, update, left_new, right_new):
    width = got.shape[2]
    mine = left_stats.shape[1]
    extra = got[0, -16:, :].astype(f32)
    grad_sq = jnp.sum(extra[1:4], keepdims=True)
    dir_sq = jnp.sum(extra[4:7], keepdims=True)
    layer_sq = jnp.sum(extras[...].astype(f32)[:, 7:10], axis=(0, 1), keepdims=True)[0]
    layer_sq = jnp.sum(layer_sq, keepdims=True)
    factor = jnp.sqrt(grad_sq / dir_sq) / jnp.sqrt(layer_sq / size)
    update[0] = (got[0, :BLOCK, :].astype(f32) * factor).astype(bf16)
    outer = got[0, BLOCK:-16, :].astype(f32) * ((1.0 - stat_decay) / width)
    for piece in range(BLOCK // width):
        columns = pl.ds(piece * width, width)
        left_new[0, :, columns] = (
            stat_decay * left_stats[0, :, columns] + outer[piece * mine : (piece + 1) * mine]
        )
    right_new[0] = stat_decay * right_stats[0] + ((1.0 - stat_decay) / BLOCK) * extra[:1]


def finish(got, left_stats, right_stats, size):
    blocks, rows, width = got.shape

    def whole(shape):
        return pl.BlockSpec((1, *shape[1:]), lambda block: (block, 0, 0))

    shapes = (
        jax.ShapeDtypeStruct((blocks, BLOCK, width), bf16),
        jax.ShapeDtypeStruct(left_stats.shape, f32),
        jax.ShapeDtypeStruct(right_stats.shape, f32),
    )
    return pl.pallas_call(
        lambda *refs: finish_kernel(float(size), *refs),
        grid=(blocks,),
        in_specs=[
            whole(got.shape),
            pl.BlockSpec((blocks, 16, width), lambda block: (0, rows // 16 - 1, 0)),
            whole(left_stats.shape),
            whole(right_stats.shape),
        ],
        out_specs=[whole(shape.shape) for shape in shapes],
        out_shape=shapes,
        name="finish",
    )(got, got, left_stats, right_stats)


def shards(activations, cotangents, left_stats, right_stats, left_roots, right_roots):
    ny = lax.axis_size("y")
    nfar = lax.axis_size("far")
    nmid = lax.axis_size("mid")
    npair = lax.axis_size("pair")
    nz = nfar * nmid * npair
    tensors = lax.axis_size("tensor")
    y = lax.axis_index("y")
    z = lax.axis_index(Z)
    pair = lax.axis_index("pair")
    place = y * npair + pair
    features = activations.shape[1]
    width = cotangents.shape[1]
    blocks = features // BLOCK
    mine = left_roots.shape[2]
    root_rows = mine * (BLOCK // width)

    half = BLOCK // npair
    partial = sum_tokens(activations, cotangents).astype(bf16)
    partial = partial.reshape(blocks * npair, half, width)
    partial, roots = lax.optimization_barrier((partial, left_roots[0].astype(bf16)))
    roots = lax.all_gather(roots, "far")
    got, roots = lax.optimization_barrier((swap(partial, ("y", "pair")), roots))
    kept = sum_tokens(lax.dynamic_slice_in_dim(activations, place * half, half, 1), cotangents)
    others = jnp.arange(ny * npair) == place
    others = jnp.where(others[:, None, None], 0.0, got.astype(f32))
    column_part = kept + jnp.sum(others, axis=0)

    got = swap(column_part.astype(bf16).reshape(nmid, half // nmid, width), "mid")
    part = jnp.sum(got.astype(f32), axis=0).astype(bf16)
    part, roots = lax.optimization_barrier((part, roots))
    held = [lax.dynamic_index_in_dim(roots, y, 1, keepdims=False)]
    for step in range(1, ny):
        turn = [(i, (i - step) % ny) for i in range(ny)]
        block = lax.dynamic_index_in_dim(roots, (y - step) % ny, 1, keepdims=False)
        held.append(lax.ppermute(block, "y", turn))
    roots = lax.dynamic_slice_in_dim(jnp.stack(held + held), (ny - y) % ny, ny, 0)
    roots = roots.reshape(ny * nfar * mine, BLOCK)
    got, roots = lax.optimization_barrier((everyone(part, "far"), roots))
    own = jnp.sum(got.astype(f32), axis=0).astype(bf16)
    gradient = everyone(own, ("pair", "mid")).reshape(BLOCK, width)

    inner = lax.dot_general(
        gradient, gradient, (((0,), (0,)), ((), ())), preferred_element_type=f32
    )
    wide = gradient.astype(f32)
    grad_sq = jnp.sum(wide * wide, axis=0)
    block_sq = jnp.sum(lax.all_gather(grad_sq, "tensor"), axis=0)

    right = lax.dynamic_index_in_dim(right_roots[0], y, 0, keepdims=False)
    mixed = jnp.dot(roots, gradient, preferred_element_type=f32)
    direction = jnp.dot(mixed, right, precision=highest).astype(bf16)
    direction = everyone(direction, ("mid", "pair")).reshape(nmid * npair, ny, nfar, mine, width)
    direction = direction.transpose(1, 2, 0, 3, 4).reshape(BLOCK, width)
    wide = direction.astype(f32)
    dir_sq = jnp.sum(wide * wide, axis=0)

    rows = lax.dynamic_index_in_dim(gradient.reshape(ny, nz, mine, width), z, 1, keepdims=False)
    outer = lax.dot_general(
        rows.reshape(ny * mine, width), gradient, (((1,), (1,)), ((), ())), preferred_element_type=f32
    )
    outer = outer.astype(bf16).reshape(ny, mine, BLOCK // width, width)
    outer = outer.transpose(0, 2, 1, 3).reshape(ny, root_rows, width)
    inner = lax.dynamic_index_in_dim(inner.reshape(ny, nz, width), z, 1, keepdims=True).astype(bf16)
    line = jnp.arange(16)[:, None]
    extra = jnp.broadcast_to(inner, (ny, 16, width))
    for place, values in enumerate(thirds(grad_sq) + thirds(dir_sq) + thirds(block_sq), 1):
        extra = jnp.where(line == place, values, extra)
    got = swap(
        jnp.concatenate(
            [jnp.broadcast_to(direction[None], (ny, BLOCK, width)), outer, extra], axis=1
        ),
        "y",
    )
    update, left_new, right_new = finish(
        got, left_stats[0], right_stats[0], features * width * tensors
    )
    return (update.reshape(blocks * BLOCK, width), left_new[None], right_new[None])


def solution(mesh):
    dp, tensor = mesh.devices.shape
    blocks, mid, pair = 4, 4, 2
    fine = Mesh(
        mesh.devices.reshape(blocks, dp // (blocks * mid * pair), mid, pair, tensor),
        ("y", "far", "mid", "pair", "tensor"),
    )
    dp = ("y", *Z)
    in_specs = (
        P(dp, None),
        P(dp, "tensor"),
        P("tensor", None, dp, None),
        P("tensor", None, dp, None),
        P("tensor", None, dp, None),
        P("tensor", None, None, None),
    )
    out_specs = (P(None, "tensor"), P("tensor", None, dp, None), P("tensor", None, dp, None))
    return jax.shard_map(shards, mesh=fine, in_specs=in_specs, out_specs=out_specs, check_vma=False)
```

```python
import jax
import jax.numpy as jnp
from jax import lax
from jax.sharding import Mesh, PartitionSpec as P

BLOCK = 1024
stat_decay = 0.95
highest = lax.Precision.HIGHEST
f32 = jnp.float32
bf16 = jnp.bfloat16
Z = ("far", "mid", "pair")


def swap(pieces, axis):
    return lax.all_to_all(pieces, axis, 0, 0, tiled=True)


def everyone(piece, axis):
    return swap(jnp.broadcast_to(piece[None], (lax.axis_size(axis), *piece.shape)), axis)


def thirds(value):
    parts = []
    for _ in range(3):
        part = lax.reduce_precision(value, 8, 7)
        parts.append(part.astype(bf16))
        value = value - part
    return parts


def sum_tokens(rows, columns):
    return lax.dot_general(rows, columns, (((0,), (0,)), ((), ())), preferred_element_type=f32)


def shards(activations, cotangents, left_stats, right_stats, left_roots, right_roots):
    ny = lax.axis_size("y")
    nfar = lax.axis_size("far")
    nmid = lax.axis_size("mid")
    npair = lax.axis_size("pair")
    nz = nfar * nmid * npair
    tensors = lax.axis_size("tensor")
    y = lax.axis_index("y")
    z = lax.axis_index(Z)
    pair = lax.axis_index("pair")
    place = y * npair + pair
    features = activations.shape[1]
    width = cotangents.shape[1]
    blocks = features // BLOCK
    mine = left_roots.shape[2]
    root_rows = mine * (BLOCK // width)

    half = BLOCK // npair
    partial = sum_tokens(activations, cotangents).astype(bf16)
    partial = partial.reshape(blocks * npair, half, width)
    partial, roots = lax.optimization_barrier((partial, left_roots[0].astype(bf16)))
    roots = lax.all_gather(roots, "far")
    got, roots = lax.optimization_barrier((swap(partial, ("y", "pair")), roots))
    kept = sum_tokens(lax.dynamic_slice_in_dim(activations, place * half, half, 1), cotangents)
    others = jnp.arange(ny * npair) == place
    others = jnp.where(others[:, None, None], 0.0, got.astype(f32))
    column_part = kept + jnp.sum(others, axis=0)

    got = swap(column_part.astype(bf16).reshape(nmid, half // nmid, width), "mid")
    part = jnp.sum(got.astype(f32), axis=0).astype(bf16)
    part, roots = lax.optimization_barrier((part, roots))
    held = [lax.dynamic_index_in_dim(roots, y, 1, keepdims=False)]
    for step in range(1, ny):
        turn = [(i, (i - step) % ny) for i in range(ny)]
        block = lax.dynamic_index_in_dim(roots, (y - step) % ny, 1, keepdims=False)
        held.append(lax.ppermute(block, "y", turn))
    roots = lax.dynamic_slice_in_dim(jnp.stack(held + held), (ny - y) % ny, ny, 0)
    roots = roots.reshape(ny * nfar * mine, BLOCK)
    got, roots = lax.optimization_barrier((everyone(part, "far"), roots))
    own = jnp.sum(got.astype(f32), axis=0).astype(bf16)
    gradient = everyone(own, ("pair", "mid")).reshape(BLOCK, width)

    inner = lax.dot_general(
        gradient, gradient, (((0,), (0,)), ((), ())), preferred_element_type=f32
    )
    wide = gradient.astype(f32)
    grad_sq = jnp.sum(wide * wide, axis=0)

    right = lax.dynamic_index_in_dim(right_roots[0], y, 0, keepdims=False)
    mixed = jnp.dot(roots, gradient, preferred_element_type=f32)
    direction = jnp.dot(mixed, right, precision=highest).astype(bf16)
    direction = everyone(direction, ("mid", "pair")).reshape(nmid * npair, ny, nfar, mine, width)
    direction = direction.transpose(1, 2, 0, 3, 4).reshape(BLOCK, width)
    wide = direction.astype(f32)
    dir_sq = jnp.sum(wide * wide, axis=0)

    rows = lax.dynamic_index_in_dim(gradient.reshape(ny, nz, mine, width), z, 1, keepdims=False)
    outer = lax.dot_general(
        rows.reshape(ny * mine, width), gradient, (((1,), (1,)), ((), ())), preferred_element_type=f32
    )
    outer = outer.astype(bf16).reshape(ny, root_rows, width)
    inner = lax.dynamic_index_in_dim(inner.reshape(ny, nz, width), z, 1, keepdims=True).astype(bf16)
    line = jnp.arange(16)[:, None]
    extra = jnp.broadcast_to(inner, (ny, 16, width))
    for place, values in enumerate(thirds(grad_sq) + thirds(dir_sq), 1):
        extra = jnp.where(line == place, values, extra)
    sent = jnp.concatenate(
        [jnp.broadcast_to(direction[None], (ny, BLOCK, width)), outer, extra], axis=1
    )
    sent, layer_sq = lax.optimization_barrier((sent, grad_sq))
    layer_sq = lax.all_gather(layer_sq, ("y", "tensor"))
    got, layer_sq = lax.optimization_barrier((swap(sent, "y"), layer_sq))
    extra = got[:, BLOCK + root_rows :].astype(f32)
    grad_sq, dir_sq = (
        jnp.sum(extra[:, 1 + 3 * n : 4 + 3 * n], axis=(1, 2), keepdims=True) for n in range(2)
    )
    layer_sq = jnp.sum(layer_sq)
    factor = jnp.sqrt(grad_sq / dir_sq) / jnp.sqrt(layer_sq / (features * width * tensors))
    update = (got[:, :BLOCK].astype(f32) * factor).astype(bf16)
    update = update.reshape(blocks * BLOCK, width)
    outer = got[:, BLOCK : BLOCK + root_rows].astype(f32).reshape(blocks, mine, BLOCK)
    left_new = stat_decay * left_stats + ((1.0 - stat_decay) / width) * outer[None]
    right_new = stat_decay * right_stats + ((1.0 - stat_decay) / BLOCK) * extra[None, :, :1]
    return (update, left_new, right_new)


def solution(mesh):
    dp, tensor = mesh.devices.shape
    blocks, mid, pair = 4, 4, 2
    fine = Mesh(
        mesh.devices.reshape(blocks, dp // (blocks * mid * pair), mid, pair, tensor),
        ("y", "far", "mid", "pair", "tensor"),
    )
    dp = ("y", *Z)
    in_specs = (
        P(dp, None),
        P(dp, "tensor"),
        P("tensor", None, dp, None),
        P("tensor", None, dp, None),
        P("tensor", None, dp, None),
        P("tensor", None, None, None),
    )
    out_specs = (P(None, "tensor"), P("tensor", None, dp, None), P("tensor", None, dp, None))
    return jax.shard_map(shards, mesh=fine, in_specs=in_specs, out_specs=out_specs, check_vma=False)
```
